32 devices in a mesh: groups: 2 (over x), seq: 16 (over z, y, core).
Axes of the slice: x: 2, y: 2, z: 4, core: 2. Of those that a mesh axis runs over, the one named last changes fastest.
Arguments:
- projected: bfloat16 [12288, 3072], P(('groups', 'seq')), parts along dimension 0, may hold values from -6 to 6
- conv_weight: float32 [3, 3072], replicated, may hold values from -3 to 3
- doc_lengths: int32 [64], P('groups'), parts along dimension 0, may hold values from 1 to 1536, 4096 in all
- load_starts: int32 [32], P('groups'), parts along dimension 0, may hold values from 0 to 3904, as said below
Outputs:
- layer_out: bfloat16 [12288, 2048], P(('groups', 'seq')), parts along dimension 0
The draws below stay inside these ranges and needn't reach their ends.
There are 2 independent parts, one for each index of `groups`. The reference program is written for one: setup_inputs(seed, part) draws one part's arguments, and reference() takes and returns one part's arrays. A program takes and returns all parts, laid end to end along the dimension named above; an argument that names none is the same for every part. Nothing has to cross between parts.
Inputs may be any that keep to these rules, and one draw needn't show every extreme that they name: load_starts[0] = 0 and load_starts rises; shard r holds the tokens load_starts[r] to load_starts[r + 1] - 1 (the last shard up to 4095), between 128 and 384 of them, and exactly 384 on some shard; load_starts[r] differs from r * 256 by at most 64, and by exactly 64 in each direction for some shard; the last entry is the largest. `doc_lengths`: the lengths sum to 4096.
All inputs are finite; a program needn't handle non-finite values.
Results may differ from the reference program's by a relative error of at most 0.0059.
Values may be sent and summed in bfloat16 or wider, within the bound.
A program may use at most 256 MiB of HBM per device.

```python
import math
import jax
import jax.numpy as jnp
import numpy as np
from jax import lax

HEADS = 32
FEAT = 16
HEAD_DIM = 64
CONV = 3
CAP = 256
EDGE = 64
TOK_DEV = 384
STREAM = 4096
TOKENS = 6144
NDOCS = 32
MOSTDOC = 1536
TAYLOR = 153
CHAN = 3072
N_SEQ = 16


def draw_load_starts(key, part):
    first_key, second_key = jax.random.split(key)
    drift_walk = jax.random.randint(first_key, (N_SEQ,), -EDGE, EDGE + 1, dtype=jnp.int32)
    marker = jax.random.randint(second_key, (), 1, N_SEQ - 1, dtype=jnp.int32)
    positions = jnp.arange(N_SEQ, dtype=jnp.int32)
    drift_walk = jnp.where(positions == N_SEQ - 2, -EDGE, drift_walk)
    drift_walk = jnp.where(positions == marker - 1, EDGE, drift_walk)
    drift_walk = jnp.where(positions == marker, -EDGE, drift_walk)
    drift_walk = jnp.where(positions == N_SEQ - 1, 0, drift_walk)
    shifted = jnp.concatenate([jnp.zeros((1,), jnp.int32), drift_walk[:-1]])
    return (positions * CAP - shifted).astype(jnp.int32)


def block_scale(own_key, dims, shards, least, top_value):
    gain = 1.0
    for axis_at, parts in shards:
        heights = jax.random.uniform(jax.random.fold_in(jax.random.fold_in(own_key, 6), axis_at), (parts,), jnp.float32, least / len(shards), top_value / len(shards))
        gain = gain * jnp.repeat(jnp.exp(heights), dims[axis_at] // parts).reshape((-1,) + (1,) * (len(dims) - 1 - axis_at))
    return gain


def length_profile(number_of, total, reach, lean):
    portions = [(1 << 20) // math.isqrt(standing ** lean) + 1 for standing in range(2, number_of + 1)]
    rest, holding = total - reach - (number_of - 1), [1] * (number_of - 1)
    while rest > 0:
        candidates = [i for i in range(number_of - 1) if holding[i] < reach]
        pool, budget = sum([portions[i] for i in candidates]), rest
        for i in candidates:
            more = min(reach - holding[i], max(1, budget * portions[i] // pool), rest)
            holding[i] = holding[i] + more
            rest = rest - more
    return np.array([reach] + holding)


def ragged_sizes(rng, count, total, most, lean):
    if count == 2:
        one = jax.random.randint(rng, (), max(1, total - most), min(most, total - 1) + 1)
        return jnp.stack([one, total - one])
    lengths = jnp.asarray(length_profile(count, total, most, lean), jnp.int32)
    pairs = (count - 1) // 2
    giver, taker = lengths[1:1 + 2 * pairs:2], lengths[2:2 + 2 * pairs:2]
    slack = jnp.minimum(giver - 1, most - taker)
    moved = jax.random.randint(jax.random.fold_in(rng, 1), (pairs,), 0, 1 << 20) % (slack + 1)
    lengths = lengths.at[1:1 + 2 * pairs:2].set(giver - moved).at[2:2 + 2 * pairs:2].set(taker + moved)
    return lengths[jax.random.permutation(jax.random.fold_in(rng, 2), count)]


def bell_draw(stream_key, shape, spread, bound, shards=(), kind=jnp.bfloat16):
    factor_of = block_scale(stream_key, shape, shards, -0.22, 0.18) if shards else 1.0
    drawn = jax.random.normal(stream_key, shape, jnp.float32) * spread * factor_of
    return jnp.minimum(jnp.maximum(drawn, -bound), bound).astype(kind)


def setup_inputs(seed: int = 0, part: int = 0) -> dict:
    key_list = jax.random.split(jax.random.key(seed), 5)
    part_splits = jax.random.split(jax.random.fold_in(key_list[4], part), 5)
    projected = bell_draw(part_splits[0], (TOKENS, CHAN), 1.0, 6.0, ((0, 16),))
    conv_weight = bell_draw(key_list[1], (CONV, CHAN), 0.6, 3.0, (), jnp.float32)
    doc_lengths = ragged_sizes(part_splits[2], NDOCS, STREAM, MOSTDOC, 1).astype(jnp.int32)
    load_starts = draw_load_starts(jax.random.fold_in(jax.random.fold_in(key_list[4], part), 71), part)
    return dict(projected=projected, conv_weight=conv_weight, doc_lengths=doc_lengths, load_starts=load_starts)


highest = lax.Precision.HIGHEST


def taylor_map(features_in):
    feat_width = features_in.shape[-1]
    upper_a, upper_b = np.triu_indices(feat_width)
    pair_scale = np.where(upper_a == upper_b, (2.0 * feat_width) ** -0.5, feat_width ** -0.5).astype(np.float32)
    constant_term = jnp.ones(features_in.shape[:-1] + (1,), features_in.dtype)
    second = features_in[..., upper_a] * features_in[..., upper_b] * pair_scale
    return jnp.concatenate([constant_term, features_in * feat_width ** -0.25, second], axis=-1)


def doc_start_of(row_ranks, doc_starts):
    inside = doc_starts[None, :] <= row_ranks[:, None]
    return jnp.max(jnp.where(inside, doc_starts[None, :], -1), axis=1).astype(jnp.int32)


def reference(projected, conv_weight, doc_lengths, load_starts):
    stream_length = N_SEQ * CAP
    rim_width = CONV - 1
    value_cols = HEADS * HEAD_DIM
    key_cols = HEADS * FEAT
    doc_starts = (jnp.cumsum(doc_lengths) - doc_lengths).astype(jnp.int32)

    def arrival_rows(row_ranks):
        owner_shard = jnp.sum((load_starts[None, :] <= row_ranks[:, None]).astype(jnp.int32), axis=1).astype(jnp.int32) - 1
        return (owner_shard * TOK_DEV + row_ranks - load_starts[owner_shard]).astype(jnp.int32)

    def block_step(carried, block_index):
        prior_state, prior_norm = carried
        first_rank = (block_index * CAP).astype(jnp.int32)
        wide_ranks = (first_rank - rim_width + jnp.arange(CAP + rim_width, dtype=jnp.int32)).astype(jnp.int32)
        wide_rows = projected[arrival_rows(jnp.maximum(wide_ranks, 0))].astype(jnp.float32)
        row_ranks = wide_ranks[rim_width:]
        row_starts = doc_start_of(row_ranks, doc_starts)
        summed = jnp.zeros((CAP, CHAN), jnp.float32)
        for offset in range(CONV):
            inside_doc = (row_ranks - offset >= row_starts)[:, None]
            shifted = wide_rows[rim_width - offset: rim_width - offset + CAP]
            summed = summed + jnp.where(inside_doc, shifted * conv_weight[offset][None, :], 0.0)
        mixed = summed.astype(jnp.bfloat16)
        query_rows = mixed[:, :key_cols].reshape(CAP, HEADS, FEAT).astype(jnp.float32)
        key_rows = mixed[:, key_cols:2 * key_cols].reshape(CAP, HEADS, FEAT).astype(jnp.float32)
        value_rows = mixed[:, 2 * key_cols:].reshape(CAP, HEADS, HEAD_DIM).astype(jnp.float32)
        same_doc = (row_ranks[None, :] <= row_ranks[:, None]) & (row_starts[None, :] == row_starts[:, None])
        scores = jnp.einsum('thf,uhf->htu', query_rows, key_rows, precision=highest) * FEAT ** -0.5
        weights = jnp.where(same_doc[None], 1.0 + scores + 0.5 * scores * scores, 0.0)
        numerator = jnp.einsum('htu,uhe->hte', weights, value_rows, precision=highest)
        denominator = jnp.sum(weights, axis=2)
        query_features = taylor_map(query_rows)
        key_features = taylor_map(key_rows)
        from_prior = (row_starts < first_rank).astype(jnp.float32)
        numerator = numerator + from_prior[None, :, None] * jnp.einsum('thf,hfe->hte', query_features, prior_state, precision=highest)
        denominator = denominator + from_prior[None, :] * jnp.einsum('thf,hf->ht', query_features, prior_norm, precision=highest)
        attended = (numerator / denominator[:, :, None]).transpose(1, 0, 2).reshape(CAP, value_cols).astype(jnp.bfloat16)
        last_start = jnp.max(row_starts)
        in_tail = (row_starts == last_start).astype(jnp.float32)
        has_start = (last_start >= first_rank).astype(jnp.float32)
        tail_keys = key_features * in_tail[:, None, None]
        local_state = jnp.einsum('thf,the->hfe', tail_keys, value_rows, precision=highest)
        local_norm = jnp.sum(tail_keys, axis=0)
        next_state = prior_state * (1.0 - has_start) + local_state
        next_norm = prior_norm * (1.0 - has_start) + local_norm
        return (next_state, next_norm), attended

    initial = (jnp.zeros((HEADS, TAYLOR, HEAD_DIM), jnp.float32), jnp.zeros((HEADS, TAYLOR), jnp.float32))
    final_state, blocks_out = lax.scan(block_step, initial, jnp.arange(N_SEQ, dtype=jnp.int32))
    attended = blocks_out.reshape(stream_length, value_cols)
    all_ranks = jnp.arange(stream_length, dtype=jnp.int32)
    placed = jnp.zeros((TOKENS, value_cols), jnp.bfloat16).at[arrival_rows(all_ranks)].set(attended)
    return placed
```

```python
import functools

import jax
import jax.numpy as jnp
from jax import lax
from jax.experimental import pallas as pl
from jax.experimental.pallas import tpu as pltpu
from jax.sharding import PartitionSpec as P

HEADS = 32
FEAT = 16
HEAD_DIM = 64
CAP = 256
PLANE = 4
KEYS = HEADS * FEAT
PAIRS = HEADS // 2
PER = PAIRS // PLANE
ROWS = 160
MESH = pl.DeviceIdType.MESH
F32 = jnp.float32
BF16 = jnp.bfloat16


def lanes(index, width=128):
    return pl.ds(pl.multiple_of(index * 128, 128), width)


def features(x, one, two):
    parts = [x * x]
    scaled = x * two
    for d in range(1, FEAT // 2):
        parts.append(scaled * pltpu.roll(x, d, 0))
    parts.append(scaled)
    parts.append(scaled[:8] * x[8:])
    row = lax.broadcasted_iota(jnp.int32, (8, x.shape[1]), 0)
    parts.append(jnp.where(row == 0, one, 0.0))
    return jnp.concatenate(parts, axis=0)


def kernel(n, proj, conv_w, doc_len, starts, out, mixed, key_t, query_t, m1, m2, tail,
           prior, valid_cols, causal, tail_rows, halo, local, from_plane, total, from_z,
           carry_out, carried, norm, acc, phi_q, halo_sem, a_send, a_recv, b_send, b_recv,
           c_send, c_recv):
    length = proj.shape[0]
    channels = proj.shape[1]
    me = lax.axis_index("seq")
    z, j = me // PLANE, me % PLANE
    planes = n // PLANE
    base = z * PLANE

    def signal(target):
        pl.semaphore_signal(barrier, inc=1, device_id={"seq": target}, device_id_type=MESH)

    def one_if(cond):
        return jnp.where(cond, 1, 0)

    barrier = pltpu.get_barrier_semaphore()
    for d in range(1, PLANE):
        signal(base + (j + d) % PLANE)
    edges = [
        (z >= 1, me - PLANE), (z >= 2, me - 2 * PLANE),
        (z < planes - 1, me + PLANE), (z < planes - 2, me + 2 * PLANE),
        ((j == PLANE - 1) & (z < planes - 1), me + 1), ((j == 0) & (z >= 1), me - 1),
    ]
    expected = PLANE - 1
    for cond, target in edges:
        pl.when(cond)(functools.partial(signal, target))
        expected = expected + one_if(cond)

    def start_of(r):
        return jnp.where(r < n, starts[jnp.minimum(jnp.maximum(r, 0), n - 1)], n * CAP)

    own = starts[me]
    after = start_of(me + 1)
    count = after - own
    edge = [start_of(base + i) for i in range(-PLANE, PLANE + 1)]

    row16 = lax.broadcasted_iota(jnp.int32, (16, channels), 0)
    token = lax.broadcasted_iota(jnp.int32, (16, length), 1)
    order = lax.broadcasted_iota(jnp.int32, (16, length), 0)
    last_two = (token == count - 2 + order) & (order < 2)
    pick_last = jnp.where(last_two, 1.0, 0.0).astype(BF16)

    def pick(tile, _):
        at = lanes(tile * 4, 512)
        tail_rows[:, at] = jnp.dot(
            pick_last, proj[:, at], preferred_element_type=F32).astype(BF16)
        return 0

    lax.fori_loop(0, channels // 512, pick, 0)

    pl.semaphore_wait(barrier, expected)
    halo_copy = pltpu.make_async_remote_copy(
        src_ref=tail_rows, dst_ref=halo, send_sem=halo_sem.at[0], recv_sem=halo_sem.at[1],
        device_id={"seq": me + 1}, device_id_type=MESH)
    pl.when(me < n - 1)(halo_copy.start)

    @pl.when(me == 0)
    def _():
        halo[...] = jnp.zeros_like(halo)

    @pl.when(z < 1)
    def _():
        from_z[0] = jnp.zeros_like(from_z[0])

    @pl.when(z < 2)
    def _():
        from_z[1] = jnp.zeros_like(from_z[1])

    slot_row = lax.broadcasted_iota(jnp.int32, (8, length), 1)
    rank_row = slot_row + own

    def doc(i, state):
        begin, row_start, last, opens = state
        row_start = jnp.where(begin <= rank_row, begin, row_start)
        last = jnp.where(begin < after, begin, last)
        opens = tuple(
            jnp.where(begin < edge[k + PLANE], begin, o) for k, o in enumerate(opens))
        return begin + doc_len[i], row_start, last, opens

    zero = jnp.int32(0)
    _, row_start, last, opens = lax.fori_loop(
        0, doc_len.shape[0], doc,
        (zero, jnp.zeros((8, length), jnp.int32), zero, (zero,) * (PLANE + 1)))
    start_row = row_start.astype(F32)[:1]
    start_col = jnp.broadcast_to(start_row, (128, length)).T
    slot_col = lax.broadcasted_iota(jnp.int32, (length, 128), 0)
    rank_col = (slot_col + own).astype(F32)
    valid_col = slot_col < count
    m1[...] = jnp.where(rank_col - 1.0 >= start_col, 1.0, 0.0)
    m2[...] = jnp.where(rank_col - 2.0 >= start_col, 1.0, 0.0)
    tail[...] = jnp.where(valid_col & (start_col == last.astype(F32)), 1.0, 0.0).astype(BF16)
    valid_row = slot_row < count
    prior[...] = jnp.where(valid_row & (row_start < own), 1.0, 0.0)
    for i in range(length // 128):
        part = slice(i * 128, i * 128 + 128)
        u = lax.broadcasted_iota(jnp.int32, (length, 128), 1) + i * 128
        same = (start_col == start_row[:, part]) & (u <= slot_col) & valid_col
        causal[:, part] = jnp.where(same, 1.0, 0.0).astype(BF16)

    def conv(tile, _):
        at = lanes(tile)
        x = proj[:, at].astype(F32)
        total_ = x * conv_w[0:1, at]
        total_ = total_ + pltpu.roll(x, 1, 0) * conv_w[1:2, at] * m1[...]
        total_ = total_ + pltpu.roll(x, 2, 0) * conv_w[2:3, at] * m2[...]
        mixed[:, at] = total_.astype(BF16)
        return 0

    def conv_edge():
        x = proj[0:16, :].astype(F32)
        before = halo[...].astype(F32)
        x1 = jnp.where(row16 < 1, pltpu.roll(before, 15, 0), pltpu.roll(x, 1, 0))
        x2 = jnp.where(row16 < 2, before, pltpu.roll(x, 2, 0))
        total_ = x * conv_w[0:1, :]
        total_ = total_ + x1 * conv_w[1:2, :] * m1[0:16, :1]
        total_ = total_ + x2 * conv_w[2:3, :] * m2[0:16, :1]
        mixed[0:16, :] = total_.astype(BF16)

    lax.fori_loop(0, channels // 128, conv, 0)
    pl.when(me > 0)(halo_copy.wait_recv)
    conv_edge()

    def turn_keys(tile, _):
        at = lanes(tile + KEYS // 128)
        key_t[lanes(tile), :] = mixed[:, at].astype(F32).T
        return 0

    lax.fori_loop(0, KEYS // 128, turn_keys, 0)

    lane = lax.broadcasted_iota(jnp.int32, (1, 128), 1)
    low = lane < 64

    def values_at(pair):
        return mixed[:, lanes(pair + 2 * KEYS // 128)]

    def state_pair(d, chunk, pp):
        pair = chunk * PER + pp
        v = values_at(pair) * tail[...]
        keys = key_t[pl.ds(pl.multiple_of(pair * 32, 32), 32), :]
        s_even = jnp.dot(features(keys[:16], 1.0, 1.0).astype(BF16),
                         jnp.where(low, v, tail[...]), preferred_element_type=F32)
        s_odd = jnp.dot(features(keys[16:], 1.0, 1.0).astype(BF16),
                        jnp.where(low, tail[...], v), preferred_element_type=F32)
        local[d, :, lanes(pp)] = jnp.where(low, s_even, s_odd).astype(BF16)
        norm[...] = jnp.where(lane == pp + 64, s_even, jnp.where(lane == pp, s_odd, norm[...]))

    a_copies = {}
    for d in (1, 2, 3, 0):
        chunk = (j + d) % PLANE
        norm[...] = jnp.zeros_like(norm)

        def step(pp, _, d=d, chunk=chunk):
            state_pair(d, chunk, pp)
            return 0

        lax.fori_loop(0, PER, step, 0)
        local[d, :, PER * 128:] = norm[...].astype(BF16)
        if d:
            a_copies[d] = pltpu.make_async_remote_copy(
                src_ref=local.at[d], dst_ref=from_plane.at[d], send_sem=a_send.at[d],
                recv_sem=a_recv.at[d], device_id={"seq": base + chunk}, device_id_type=MESH)
            a_copies[d].start()

    def turn_queries(tile, _):
        at = lanes(tile)
        scaled = mixed[:, at].astype(F32) * 0.25
        mixed[:, at] = scaled.astype(BF16)
        query_t[at, :] = scaled.T
        return 0

    lax.fori_loop(0, KEYS // 128, turn_queries, 0)

    def query_features(head, _):
        q = query_t[pl.ds(pl.multiple_of(head * 16, 16), 16), :]
        phi = features(q, 2.0, 2.0) * prior[0:1, :]
        phi = jnp.concatenate([phi, jnp.zeros((256 - ROWS, length), F32)], axis=0)
        phi_q[head] = phi.astype(BF16).T
        return 0

    lax.fori_loop(0, HEADS // 2, query_features, 0)

    def gathered(d):
        return local[0] if d == 0 else from_plane[d]

    for d in range(1, PLANE):
        a_copies[d].wait_recv()
    total_sum = jnp.zeros(total.shape, F32)
    for d in range(PLANE):
        source = (j - d + PLANE) % PLANE
        keep = jnp.where(opens[PLANE] < start_of(base + source + 1), 1.0, 0.0)
        total_sum = total_sum + gathered(d).astype(F32) * keep
    total[...] = total_sum.astype(BF16)
    b_copies = []
    for k in (1, 2):
        b_copies.append(pltpu.make_async_remote_copy(
            src_ref=total, dst_ref=from_z.at[k - 1], send_sem=b_send.at[k - 1],
            recv_sem=b_recv.at[k - 1], device_id={"seq": me + k * PLANE}, device_id_type=MESH))
        pl.when(z < planes - k)(b_copies[-1].start)

    lax.fori_loop(HEADS // 2, HEADS, query_features, 0)

    key_row = lax.broadcasted_iota(jnp.int32, (128, 1), 0) // FEAT
    half = 256
    def attend(pair, _):
        tile = pair // 4
        v = values_at(pair)
        q = mixed[:, lanes(tile)]
        keys = key_t[lanes(tile), :]
        one = jnp.ones_like(v)
        for side in range(2):
            here = (pair % 4) * 2 + side
            k = jnp.where(key_row == here, keys, 0.0).astype(BF16)
            va = jnp.where(low, v, one) if side == 0 else jnp.where(low, one, v)
            for lo, hi in ((0, half), (half, length)):
                s = jnp.dot(q[lo:hi], k[:, :hi], preferred_element_type=F32) + 1.0
                w = (s * s + 1.0).astype(BF16) * causal[lo:hi, :hi]
                acc[pair * 2 + side, lo:hi, :] = jnp.dot(
                    w, va[:hi], preferred_element_type=F32)
        return 0

    lax.fori_loop(0, PAIRS * 5 // 8, attend, 0)

    for k in (1, 2):
        pl.when(z >= k)(b_copies[k - 1].wait_recv)
    c_copies = {}
    for d in (1, 2, 3, 0):
        to = (j + d) % PLANE
        open_at = opens[0]
        for i in range(1, PLANE):
            open_at = jnp.where(to == i, opens[i], open_at)
        state = from_z[0].astype(F32) * jnp.where(open_at < edge[PLANE], 1.0, 0.0)
        state = state + from_z[1].astype(F32) * jnp.where(open_at < edge[0], 1.0, 0.0)
        for e in range(PLANE):
            source = (j - e + PLANE) % PLANE
            keep = (source < to) & (open_at < start_of(base + source + 1))
            state = state + gathered(e).astype(F32) * jnp.where(keep, 1.0, 0.0)
        if d:
            carry_out[d] = state.astype(BF16)
            c_copies[d] = pltpu.make_async_remote_copy(
                src_ref=carry_out.at[d], dst_ref=carried.at[d], send_sem=c_send.at[d],
                recv_sem=c_recv.at[d], device_id={"seq": base + to}, device_id_type=MESH)
            c_copies[d].start()
        else:
            carried[0] = state.astype(BF16)

    lax.fori_loop(PAIRS * 5 // 8, PAIRS, attend, 0)

    from_row = lax.broadcasted_iota(jnp.int32, (128, 256), 0)
    to_col = lax.broadcasted_iota(jnp.int32, (128, 256), 1)
    pad = jnp.zeros((256 - ROWS, 128), BF16)
    for d in range(PLANE):
        if d:
            c_copies[d].wait_recv()
        chunk = (j - d + PLANE) % PLANE

        def finish(pp, _, d=d, chunk=chunk):
            pair = chunk * PER + pp
            values = carried[d, :, lanes(pp)]
            pick = ((from_row == pp + 64) & (to_col < 128)) | ((from_row == pp) & (to_col >= 128))
            norms = jnp.dot(carried[d, :, PER * 128:], jnp.where(pick, 1.0, 0.0).astype(BF16),
                            preferred_element_type=F32).astype(BF16)
            s_even = jnp.concatenate([jnp.where(low, values, norms[:, :128]), pad], axis=0)
            s_odd = jnp.concatenate([jnp.where(low, norms[:, 128:], values), pad], axis=0)
            even = acc[pair * 2] + jnp.dot(phi_q[pair * 2], s_even, preferred_element_type=F32)
            odd = acc[pair * 2 + 1] + jnp.dot(phi_q[pair * 2 + 1], s_odd, preferred_element_type=F32)
            numer = jnp.where(low, even, odd)
            denom = pltpu.roll(jnp.where(low, odd, even), 64, 1)
            good = denom != 0.0
            result = jnp.where(good, numer / jnp.where(good, denom, 1.0), 0.0)
            out[:, lanes(pair)] = result.astype(BF16)
            return 0

        lax.fori_loop(0, PER, finish, 0)

    pl.when(me < n - 1)(halo_copy.wait_send)
    for d in range(1, PLANE):
        a_copies[d].wait_send()
        c_copies[d].wait_send()
    for k in (1, 2):
        pl.when(z < planes - k)(b_copies[k - 1].wait_send)


def per_device(projected, conv_weight, doc_lengths, load_starts):
    n = lax.axis_size("seq")
    length, channels = projected.shape
    state = (ROWS, (PER + 1) * 128)
    vmem = pl.BlockSpec(memory_space=pltpu.VMEM)
    smem = pl.BlockSpec(memory_space=pltpu.SMEM)
    return pl.pallas_call(
        functools.partial(kernel, n),
        out_shape=jax.ShapeDtypeStruct((length, HEADS * HEAD_DIM), BF16),
        in_specs=[vmem, vmem, smem, smem],
        out_specs=vmem,
        scratch_shapes=[
            pltpu.VMEM((length, channels), BF16),
            pltpu.VMEM((KEYS, length), F32),
            pltpu.VMEM((KEYS, length), F32),
            pltpu.VMEM((length, 128), F32),
            pltpu.VMEM((length, 128), F32),
            pltpu.VMEM((length, 128), BF16),
            pltpu.VMEM((8, length), F32),
            pltpu.VMEM((8, 128), F32),
            pltpu.VMEM((length, length), BF16),
            pltpu.VMEM((16, channels), BF16),
            pltpu.VMEM((16, channels), BF16),
            pltpu.VMEM((PLANE,) + state, BF16),
            pltpu.VMEM((PLANE,) + state, BF16),
            pltpu.VMEM(state, BF16),
            pltpu.VMEM((2,) + state, BF16),
            pltpu.VMEM((PLANE,) + state, BF16),
            pltpu.VMEM((PLANE,) + state, BF16),
            pltpu.VMEM((ROWS, 128), F32),
            pltpu.VMEM((HEADS, length, 128), F32),
            pltpu.VMEM((HEADS, length, 256), BF16),
            pltpu.SemaphoreType.DMA((2,)),
            pltpu.SemaphoreType.DMA((PLANE,)),
            pltpu.SemaphoreType.DMA((PLANE,)),
            pltpu.SemaphoreType.DMA((2,)),
            pltpu.SemaphoreType.DMA((2,)),
            pltpu.SemaphoreType.DMA((PLANE,)),
            pltpu.SemaphoreType.DMA((PLANE,)),
        ],
        compiler_params=pltpu.CompilerParams(
            collective_id=0, has_side_effects=True, vmem_limit_bytes=48 * 1024 * 1024),
    )(projected, conv_weight, doc_lengths, load_starts)


def solution(mesh):
    return jax.shard_map(
        per_device,
        mesh=mesh,
        in_specs=(P(("groups", "seq"), None), P(), P("groups"), P("groups")),
        out_specs=P(("groups", "seq"), None),
        check_vma=False,
    )
```

```python
import functools

import jax
import jax.numpy as jnp
from jax import lax
from jax.experimental import pallas as pl
from jax.experimental.pallas import tpu as pltpu
from jax.sharding import PartitionSpec as P

HEADS = 32
FEAT = 16
HEAD_DIM = 64
CAP = 256
PLANE = 4
KEYS = HEADS * FEAT
PAIRS = HEADS // 2
PER = PAIRS // PLANE
ROWS = 160
MESH = pl.DeviceIdType.MESH
F32 = jnp.float32
BF16 = jnp.bfloat16


def lanes(index, width=128):
    return pl.ds(pl.multiple_of(index * 128, 128), width)


def features(x, one, two):
    parts = [x * x]
    scaled = x * two
    for d in range(1, FEAT // 2):
        parts.append(scaled * pltpu.roll(x, d, 0))
    parts.append(scaled)
    parts.append(scaled[:8] * x[8:])
    row = lax.broadcasted_iota(jnp.int32, (8, x.shape[1]), 0)
    parts.append(jnp.where(row == 0, one, 0.0))
    return jnp.concatenate(parts, axis=0)


def kernel(n, proj_hbm, conv_hbm, doc_len, starts, out, proj, conv_w, mixed, key_t, query_t, m1, m2, tail,
           prior, causal, tail_rows, halo, local, from_plane, total, from_z,
           carry_out, carried, acc, phi_q, halo_sem, a_send, a_recv, b_send, b_recv,
           c_send, c_recv, load_sem):
    loads = [pltpu.make_async_copy(proj_hbm, proj, load_sem.at[0]),
             pltpu.make_async_copy(conv_hbm, conv_w, load_sem.at[1])]
    for load in loads:
        load.start()
    length = proj.shape[0]
    channels = proj.shape[1]
    me = lax.axis_index("seq")
    z, j = me // PLANE, me % PLANE
    planes = n // PLANE
    base = z * PLANE

    def signal(target):
        pl.semaphore_signal(barrier, inc=1, device_id={"seq": target}, device_id_type=MESH)

    def one_if(cond):
        return jnp.where(cond, 1, 0)

    barrier = pltpu.get_barrier_semaphore()
    for d in range(1, PLANE):
        signal(base + (j + d) % PLANE)
    edges = [
        (z >= 1, me - PLANE), (z >= 2, me - 2 * PLANE),
        (z < planes - 1, me + PLANE), (z < planes - 2, me + 2 * PLANE),
        ((j == PLANE - 1) & (z < planes - 1), me + 1), ((j == 0) & (z >= 1), me - 1),
    ]
    expected = PLANE - 1
    for cond, target in edges:
        pl.when(cond)(functools.partial(signal, target))
        expected = expected + one_if(cond)

    def start_of(r):
        return jnp.where(r < n, starts[jnp.minimum(jnp.maximum(r, 0), n - 1)], n * CAP)

    own = starts[me]
    after = start_of(me + 1)
    count = after - own
    edge = [start_of(base + i) for i in range(-PLANE, PLANE + 1)]

    row16 = lax.broadcasted_iota(jnp.int32, (16, channels), 0)
    token = lax.broadcasted_iota(jnp.int32, (16, length), 1)
    order = lax.broadcasted_iota(jnp.int32, (16, length), 0)
    last_two = (token == count - 2 + order) & (order < 2)
    pick_last = jnp.where(last_two, 1.0, 0.0).astype(BF16)

    for load in loads:
        load.wait()

    def pick(tile, _):
        at = lanes(tile * 4, 512)
        tail_rows[:, at] = jnp.dot(
            pick_last, proj[:, at], preferred_element_type=F32).astype(BF16)
        return 0

    lax.fori_loop(0, channels // 512, pick, 0)

    pl.semaphore_wait(barrier, expected)
    halo_copy = pltpu.make_async_remote_copy(
        src_ref=tail_rows, dst_ref=halo, send_sem=halo_sem.at[0], recv_sem=halo_sem.at[1],
        device_id={"seq": me + 1}, device_id_type=MESH)
    pl.when(me < n - 1)(halo_copy.start)

    @pl.when(me == 0)
    def _():
        halo[...] = jnp.zeros_like(halo)

    @pl.when(z < 1)
    def _():
        from_z[0] = jnp.zeros_like(from_z[0])

    @pl.when(z < 2)
    def _():
        from_z[1] = jnp.zeros_like(from_z[1])

    slot_row = lax.broadcasted_iota(jnp.int32, (8, length), 1)
    rank_row = slot_row + own

    def doc(i, state):
        begin, row_start, last, opens = state
        row_start = jnp.where(begin <= rank_row, begin, row_start)
        last = jnp.where(begin < after, begin, last)
        opens = tuple(
            jnp.where(begin < edge[k + PLANE], begin, o) for k, o in enumerate(opens))
        return begin + doc_len[i], row_start, last, opens

    zero = jnp.int32(0)
    _, row_start, last, opens = lax.fori_loop(
        0, doc_len.shape[0], doc,
        (zero, jnp.zeros((8, length), jnp.int32), zero, (zero,) * (PLANE + 1)))
    start_row = row_start.astype(F32)[:1]
    start_col = jnp.broadcast_to(start_row, (128, length)).T
    slot_col = lax.broadcasted_iota(jnp.int32, (length, 128), 0)
    rank_col = (slot_col + own).astype(F32)
    valid_col = slot_col < count
    m1[...] = jnp.where(rank_col - 1.0 >= start_col, 1.0, 0.0)
    m2[...] = jnp.where(rank_col - 2.0 >= start_col, 1.0, 0.0)
    tail[...] = jnp.where(valid_col & (start_col == last.astype(F32)), 1.0, 0.0).astype(BF16)
    valid_row = slot_row < count
    prior[...] = jnp.where(valid_row & (row_start < own), 1.0, 0.0)
    for i in range(length // 128):
        part = slice(i * 128, i * 128 + 128)
        u = lax.broadcasted_iota(jnp.int32, (length, 128), 1) + i * 128
        same = (start_col == start_row[:, part]) & (u <= slot_col) & valid_col
        same = jnp.where(same, 1.0, 0.0).astype(BF16)
        causal[:, i * 256:i * 256 + 128] = same
        causal[:, i * 256 + 128:i * 256 + 256] = same

    def conv(tile, _):
        at = lanes(tile)
        x = proj[:, at].astype(F32)
        total_ = x * conv_w[0:1, at]
        total_ = total_ + pltpu.roll(x, 1, 0) * conv_w[1:2, at] * m1[...]
        total_ = total_ + pltpu.roll(x, 2, 0) * conv_w[2:3, at] * m2[...]
        mixed[:, at] = total_.astype(BF16)
        return 0

    def conv_edge():
        x = proj[0:16, :].astype(F32)
        before = halo[...].astype(F32)
        x1 = jnp.where(row16 < 1, pltpu.roll(before, 15, 0), pltpu.roll(x, 1, 0))
        x2 = jnp.where(row16 < 2, before, pltpu.roll(x, 2, 0))
        total_ = x * conv_w[0:1, :]
        total_ = total_ + x1 * conv_w[1:2, :] * m1[0:16, :1]
        total_ = total_ + x2 * conv_w[2:3, :] * m2[0:16, :1]
        mixed[0:16, :] = total_.astype(BF16)

    lax.fori_loop(0, channels // 128, conv, 0)
    pl.when(me > 0)(halo_copy.wait_recv)
    conv_edge()

    def turn_keys(tile, _):
        at = lanes(tile + KEYS // 128)
        key_t[lanes(tile), :] = mixed[:, at].astype(F32).T
        return 0

    lax.fori_loop(0, KEYS // 128, turn_keys, 0)

    lane = lax.broadcasted_iota(jnp.int32, (1, 128), 1)
    low = lane < 64

    def values_at(pair):
        return mixed[:, lanes(pair + 2 * KEYS // 128)]

    def state_pair(d, chunk, pp):
        pair = chunk * PER + pp
        v = values_at(pair) * tail[...]
        keys = key_t[pl.ds(pl.multiple_of(pair * 32, 32), 32), :]
        phi = jnp.concatenate(
            [features(keys[:16], 1.0, 1.0), features(keys[16:], 1.0, 1.0)], axis=0).astype(BF16)
        both = jnp.dot(phi, jnp.concatenate([v, tail[...]], axis=1), preferred_element_type=F32)
        local[d, :, lanes(pp)] = jnp.where(low, both[:ROWS, :128], both[ROWS:, :128]).astype(BF16)
        return jnp.where(lane == pp + 64, both[:ROWS, 128:],
                         jnp.where(lane == pp, both[ROWS:, 128:], 0.0))

    a_copies = {}
    for d in (1, 2, 3, 0):
        chunk = (j + d) % PLANE
        norm = jnp.zeros((ROWS, 128), F32)
        for pp in range(PER):
            norm = norm + state_pair(d, chunk, pp)
        local[d, :, PER * 128:] = norm.astype(BF16)
        if d:
            a_copies[d] = pltpu.make_async_remote_copy(
                src_ref=local.at[d], dst_ref=from_plane.at[d], send_sem=a_send.at[d],
                recv_sem=a_recv.at[d], device_id={"seq": base + chunk}, device_id_type=MESH)
            a_copies[d].start()

    def turn_queries(tile, _):
        at = lanes(tile)
        scaled = mixed[:, at].astype(F32) * 0.25
        mixed[:, at] = scaled.astype(BF16)
        query_t[at, :] = scaled.T
        return 0

    lax.fori_loop(0, KEYS // 128, turn_queries, 0)

    def query_features(head, _):
        q = query_t[pl.ds(pl.multiple_of(head * 16, 16), 16), :]
        phi = features(q, 2.0, 2.0) * prior[0:1, :]
        phi = jnp.concatenate([phi, jnp.zeros((256 - ROWS, length), F32)], axis=0)
        phi_q[head] = phi.astype(BF16).T
        return 0

    lax.fori_loop(0, HEADS // 2, query_features, 0)

    def gathered(d):
        return local[0] if d == 0 else from_plane[d]

    for d in range(1, PLANE):
        a_copies[d].wait_recv()
    total_sum = jnp.zeros(total.shape, F32)
    for d in range(PLANE):
        source = (j - d + PLANE) % PLANE
        keep = jnp.where(opens[PLANE] < start_of(base + source + 1), 1.0, 0.0)
        total_sum = total_sum + gathered(d).astype(F32) * keep
    total[...] = total_sum.astype(BF16)
    b_copies = []
    for k in (1, 2):
        b_copies.append(pltpu.make_async_remote_copy(
            src_ref=total, dst_ref=from_z.at[k - 1], send_sem=b_send.at[k - 1],
            recv_sem=b_recv.at[k - 1], device_id={"seq": me + k * PLANE}, device_id_type=MESH))
        pl.when(z < planes - k)(b_copies[-1].start)

    lax.fori_loop(HEADS // 2, HEADS, query_features, 0)

    key_row = lax.broadcasted_iota(jnp.int32, (128, 1), 0) // FEAT
    blocks = length // 128

    def attend(pair, _):
        tile = pair // 4
        v = values_at(pair)
        q = mixed[:, lanes(tile)]
        keys = key_t[lanes(tile), :]
        here = (pair % 4) * 2
        k_even = jnp.where(key_row == here, keys, 0.0).astype(BF16)
        k_odd = jnp.where(key_row == here + 1, keys, 0.0).astype(BF16)
        one, nil = jnp.ones((128, 128), BF16), jnp.zeros((128, 128), BF16)
        sums = []
        for b in range(blocks):
            part = slice(b * 128, b * 128 + 128)
            k = jnp.concatenate([k_even[:, part], k_odd[:, part]], axis=1)
            s = jnp.dot(q[b * 128:], k, preferred_element_type=F32) + 1.0
            w = (s * s + 1.0).astype(BF16) * causal[b * 128:, b * 256:b * 256 + 256]
            va = jnp.concatenate([
                jnp.concatenate([jnp.where(low, v[part], one), nil], axis=1),
                jnp.concatenate([nil, jnp.where(low, one, v[part])], axis=1)], axis=0)
            sums.append(jnp.dot(w, va, preferred_element_type=F32))
        for b in range(blocks):
            rows = slice(b * 128, b * 128 + 128)
            whole = sums[0][rows]
            for e in range(1, b + 1):
                whole = whole + sums[e][(b - e) * 128:(b - e) * 128 + 128]
            acc[pair, rows, :] = whole
        return 0

    lax.fori_loop(0, PAIRS * 5 // 8, attend, 0, unroll=2)

    for k in (1, 2):
        pl.when(z >= k)(b_copies[k - 1].wait_recv)
    c_copies = {}
    for d in (1, 2, 3, 0):
        to = (j + d) % PLANE
        open_at = opens[0]
        for i in range(1, PLANE):
            open_at = jnp.where(to == i, opens[i], open_at)
        state = from_z[0].astype(F32) * jnp.where(open_at < edge[PLANE], 1.0, 0.0)
        state = state + from_z[1].astype(F32) * jnp.where(open_at < edge[0], 1.0, 0.0)
        for e in range(PLANE):
            source = (j - e + PLANE) % PLANE
            keep = (source < to) & (open_at < start_of(base + source + 1))
            state = state + gathered(e).astype(F32) * jnp.where(keep, 1.0, 0.0)
        if d:
            carry_out[d] = state.astype(BF16)
            c_copies[d] = pltpu.make_async_remote_copy(
                src_ref=carry_out.at[d], dst_ref=carried.at[d], send_sem=c_send.at[d],
                recv_sem=c_recv.at[d], device_id={"seq": base + to}, device_id_type=MESH)
            c_copies[d].start()
        else:
            carried[0] = state.astype(BF16)

    lax.fori_loop(PAIRS * 5 // 8, PAIRS, attend, 0, unroll=2)

    from_row = lax.broadcasted_iota(jnp.int32, (128, PER * 256), 0)
    to_col = lax.broadcasted_iota(jnp.int32, (128, PER * 256), 1)
    spread = jnp.where(
        from_row == to_col // 256 + jnp.where(to_col % 256 < 128, 64, 0), 1.0, 0.0).astype(BF16)
    pad = jnp.zeros((256 - ROWS, 128), BF16)
    for d in range(PLANE):
        if d:
            c_copies[d].wait_recv()
        chunk = (j - d + PLANE) % PLANE

        norms = jnp.dot(carried[d, :, PER * 128:], spread, preferred_element_type=F32).astype(BF16)
        for pp in range(PER):
            pair = chunk * PER + pp
            values = carried[d, :, pp * 128:pp * 128 + 128]
            norm = norms[:, pp * 256:pp * 256 + 256]
            s_even = jnp.concatenate([jnp.where(low, values, norm[:, :128]), pad], axis=0)
            s_odd = jnp.concatenate([jnp.where(low, norm[:, 128:], values), pad], axis=0)
            mine = acc[pair]
            even = mine[:, :128] + jnp.dot(phi_q[pair * 2], s_even, preferred_element_type=F32)
            odd = mine[:, 128:] + jnp.dot(phi_q[pair * 2 + 1], s_odd, preferred_element_type=F32)
            numer = jnp.where(low, even, odd)
            denom = pltpu.roll(jnp.where(low, odd, even), 64, 1)
            good = denom != 0.0
            result = jnp.where(good, numer / jnp.where(good, denom, 1.0), 0.0)
            out[:, lanes(pair)] = result.astype(BF16)

    pl.when(me < n - 1)(halo_copy.wait_send)
    for d in range(1, PLANE):
        a_copies[d].wait_send()
        c_copies[d].wait_send()
    for k in (1, 2):
        pl.when(z < planes - k)(b_copies[k - 1].wait_send)


def per_device(projected, conv_weight, doc_lengths, load_starts):
    n = lax.axis_size("seq")
    length, channels = projected.shape
    state = (ROWS, (PER + 1) * 128)
    vmem = pl.BlockSpec(memory_space=pltpu.VMEM)
    smem = pl.BlockSpec(memory_space=pltpu.SMEM)
    return pl.pallas_call(
        functools.partial(kernel, n),
        out_shape=jax.ShapeDtypeStruct((length, HEADS * HEAD_DIM), BF16),
        in_specs=[pl.BlockSpec(memory_space=pl.ANY)] * 2 + [smem, smem],
        out_specs=vmem,
        scratch_shapes=[
            pltpu.VMEM((length, channels), BF16),
            pltpu.VMEM(conv_weight.shape, F32),
            pltpu.VMEM((length, channels), BF16),
            pltpu.VMEM((KEYS, length), F32),
            pltpu.VMEM((KEYS, length), F32),
            pltpu.VMEM((length, 128), F32),
            pltpu.VMEM((length, 128), F32),
            pltpu.VMEM((length, 128), BF16),
            pltpu.VMEM((8, length), F32),
            pltpu.VMEM((length, 2 * length), BF16),
            pltpu.VMEM((16, channels), BF16),
            pltpu.VMEM((16, channels), BF16),
            pltpu.VMEM((PLANE,) + state, BF16),
            pltpu.VMEM((PLANE,) + state, BF16),
            pltpu.VMEM(state, BF16),
            pltpu.VMEM((2,) + state, BF16),
            pltpu.VMEM((PLANE,) + state, BF16),
            pltpu.VMEM((PLANE,) + state, BF16),
            pltpu.VMEM((PAIRS, length, 256), F32),
            pltpu.VMEM((HEADS, length, 256), BF16),
            pltpu.SemaphoreType.DMA((2,)),
            pltpu.SemaphoreType.DMA((PLANE,)),
            pltpu.SemaphoreType.DMA((PLANE,)),
            pltpu.SemaphoreType.DMA((2,)),
            pltpu.SemaphoreType.DMA((2,)),
            pltpu.SemaphoreType.DMA((PLANE,)),
            pltpu.SemaphoreType.DMA((PLANE,)),
            pltpu.SemaphoreType.DMA((2,)),
        ],
        compiler_params=pltpu.CompilerParams(
            collective_id=0, has_side_effects=True, vmem_limit_bytes=60 * 1024 * 1024),
    )(projected, conv_weight, doc_lengths, load_starts)


def solution(mesh):
    return jax.shard_map(
        per_device,
        mesh=mesh,
        in_specs=(P(("groups", "seq"), None), P(), P("groups"), P("groups")),
        out_specs=P(("groups", "seq"), None),
        check_vma=False,
    )
```

```python
import functools

import jax
import jax.numpy as jnp
from jax import lax
from jax.experimental import pallas as pl
from jax.experimental.pallas import tpu as pltpu
from jax.sharding import PartitionSpec as P

HEADS = 32
FEAT = 16
HEAD_DIM = 64
CAP = 256
PLANE = 4
KEYS = HEADS * FEAT
PAIRS = HEADS // 2
PER = PAIRS // PLANE
PARTS = 2
ROWS = 160
MESH = pl.DeviceIdType.MESH
F32 = jnp.float32
BF16 = jnp.bfloat16


def lanes(index, width=128):
    return pl.ds(pl.multiple_of(index * 128, 128), width)


def features(x, one, two):
    parts = [x * x]
    scaled = x * two
    for d in range(1, FEAT // 2):
        parts.append(scaled * pltpu.roll(x, d, 0))
    parts.append(scaled)
    parts.append(scaled[:8] * x[8:])
    row = lax.broadcasted_iota(jnp.int32, (8, x.shape[1]), 0)
    parts.append(jnp.where(row == 0, one, 0.0))
    return jnp.concatenate(parts, axis=0)


def kernel(n, proj_hbm, conv_hbm, doc_len, starts, out, proj, conv_w, mixed, key_t, query_t, m1, m2, tail,
           prior, causal, tail_rows, halo, local, from_plane, total, from_z,
           carry_out, carried, acc, phi_q, halo_sem, a_send, a_recv, b_send, b_recv,
           c_send, c_recv, load_sem):
    loads = [pltpu.make_async_copy(proj_hbm, proj, load_sem.at[0]),
             pltpu.make_async_copy(conv_hbm, conv_w, load_sem.at[1])]
    for load in loads:
        load.start()
    length = proj.shape[0]
    channels = proj.shape[1]
    me = lax.axis_index("seq")
    z, j = me // PLANE, me % PLANE
    planes = n // PLANE
    base = z * PLANE

    def signal(target):
        pl.semaphore_signal(barrier, inc=1, device_id={"seq": target}, device_id_type=MESH)

    def one_if(cond):
        return jnp.where(cond, 1, 0)

    barrier = pltpu.get_barrier_semaphore()
    for d in range(1, PLANE):
        signal(base + (j + d) % PLANE)
    edges = [
        (z >= 1, me - PLANE), (z >= 2, me - 2 * PLANE),
        (z < planes - 1, me + PLANE), (z < planes - 2, me + 2 * PLANE),
        ((j == PLANE - 1) & (z < planes - 1), me + 1), ((j == 0) & (z >= 1), me - 1),
    ]
    expected = PLANE - 1
    for cond, target in edges:
        pl.when(cond)(functools.partial(signal, target))
        expected = expected + one_if(cond)

    def start_of(r):
        return jnp.where(r < n, starts[jnp.minimum(jnp.maximum(r, 0), n - 1)], n * CAP)

    own = starts[me]
    after = start_of(me + 1)
    count = after - own
    edge = [start_of(base + i) for i in range(-PLANE, PLANE + 1)]

    row16 = lax.broadcasted_iota(jnp.int32, (16, channels), 0)
    token = lax.broadcasted_iota(jnp.int32, (16, length), 1)
    order = lax.broadcasted_iota(jnp.int32, (16, length), 0)
    last_two = (token == count - 2 + order) & (order < 2)
    pick_last = jnp.where(last_two, 1.0, 0.0).astype(BF16)

    for load in loads:
        load.wait()

    def pick(tile, _):
        at = lanes(tile * 4, 512)
        tail_rows[:, at] = jnp.dot(
            pick_last, proj[:, at], preferred_element_type=F32).astype(BF16)
        return 0

    lax.fori_loop(0, channels // 512, pick, 0)

    pl.semaphore_wait(barrier, expected)
    halo_copy = pltpu.make_async_remote_copy(
        src_ref=tail_rows, dst_ref=halo, send_sem=halo_sem.at[0], recv_sem=halo_sem.at[1],
        device_id={"seq": me + 1}, device_id_type=MESH)
    pl.when(me < n - 1)(halo_copy.start)

    @pl.when(me == 0)
    def _():
        halo[...] = jnp.zeros_like(halo)

    @pl.when(z < 1)
    def _():
        from_z[0] = jnp.zeros_like(from_z[0])

    @pl.when(z < 2)
    def _():
        from_z[1] = jnp.zeros_like(from_z[1])

    slot_row = lax.broadcasted_iota(jnp.int32, (8, length), 1)
    rank_row = slot_row + own

    def doc(i, state):
        begin, row_start, last, opens = state
        row_start = jnp.where(begin <= rank_row, begin, row_start)
        last = jnp.where(begin < after, begin, last)
        opens = tuple(
            jnp.where(begin < edge[k + PLANE], begin, o) for k, o in enumerate(opens))
        return begin + doc_len[i], row_start, last, opens

    zero = jnp.int32(0)
    _, row_start, last, opens = lax.fori_loop(
        0, doc_len.shape[0], doc,
        (zero, jnp.zeros((8, length), jnp.int32), zero, (zero,) * (PLANE + 1)))
    start_row = row_start.astype(F32)[:1]
    start_col = jnp.broadcast_to(start_row, (128, length)).T
    slot_col = lax.broadcasted_iota(jnp.int32, (length, 128), 0)
    rank_col = (slot_col + own).astype(F32)
    valid_col = slot_col < count
    m1[...] = jnp.where(rank_col - 1.0 >= start_col, 1.0, 0.0)
    m2[...] = jnp.where(rank_col - 2.0 >= start_col, 1.0, 0.0)
    tail[...] = jnp.where(valid_col & (start_col == last.astype(F32)), 1.0, 0.0).astype(BF16)
    valid_row = slot_row < count
    prior[...] = jnp.where(valid_row & (row_start < own), 1.0, 0.0)
    for i in range(length // 128):
        part = slice(i * 128, i * 128 + 128)
        u = lax.broadcasted_iota(jnp.int32, (length, 128), 1) + i * 128
        same = (start_col == start_row[:, part]) & (u <= slot_col) & valid_col
        same = jnp.where(same, 1.0, 0.0).astype(BF16)
        causal[:, i * 256:i * 256 + 128] = same
        causal[:, i * 256 + 128:i * 256 + 256] = same

    def conv(tile, _):
        at = lanes(tile)
        x = proj[:, at].astype(F32)
        total_ = x * conv_w[0:1, at]
        total_ = total_ + pltpu.roll(x, 1, 0) * conv_w[1:2, at] * m1[...]
        total_ = total_ + pltpu.roll(x, 2, 0) * conv_w[2:3, at] * m2[...]
        mixed[:, at] = total_.astype(BF16)
        return 0

    def conv_edge():
        x = proj[0:16, :].astype(F32)
        before = halo[...].astype(F32)
        x1 = jnp.where(row16 < 1, pltpu.roll(before, 15, 0), pltpu.roll(x, 1, 0))
        x2 = jnp.where(row16 < 2, before, pltpu.roll(x, 2, 0))
        total_ = x * conv_w[0:1, :]
        total_ = total_ + x1 * conv_w[1:2, :] * m1[0:16, :1]
        total_ = total_ + x2 * conv_w[2:3, :] * m2[0:16, :1]
        mixed[0:16, :] = total_.astype(BF16)

    lax.fori_loop(0, channels // 128, conv, 0)
    pl.when(me > 0)(halo_copy.wait_recv)
    conv_edge()

    def turn_keys(tile, _):
        at = lanes(tile + KEYS // 128)
        key_t[lanes(tile), :] = mixed[:, at].astype(F32).T
        return 0

    lax.fori_loop(0, KEYS // 128, turn_keys, 0)

    lane = lax.broadcasted_iota(jnp.int32, (1, 128), 1)
    low = lane < 64

    def values_at(pair):
        return mixed[:, lanes(pair + 2 * KEYS // 128)]

    row16_part = lax.broadcasted_iota(jnp.int32, (16, 256), 0)

    def state_part(d, chunk, h):
        ends = jnp.zeros((16, 256), F32)
        for i in range(PER // PARTS):
            pair = chunk * PER + h * (PER // PARTS) + i
            v = values_at(pair) * tail[...]
            keys = key_t[pl.ds(pl.multiple_of(pair * 32, 32), 32), :]
            phi = jnp.concatenate(
                [features(keys[:16], 1.0, 1.0), features(keys[16:], 1.0, 1.0)],
                axis=0).astype(BF16)
            both = jnp.dot(phi, jnp.concatenate([v, tail[...]], axis=1),
                           preferred_element_type=F32)
            local[d, h, :, i * 128:i * 128 + 128] = jnp.where(
                low, both[:ROWS, :128], both[ROWS:, :128]).astype(BF16)
            for side in range(2):
                column = both[side * ROWS:side * ROWS + ROWS, 128:]
                turned = jnp.concatenate(
                    [column, jnp.zeros((256 - ROWS, 128), F32)], axis=0).T[:1]
                ends = ends + jnp.where(row16_part == 9 + 2 * i + side, turned, 0.0)
        last_rows = local[d, h, ROWS - 16:, :].astype(F32)
        local[d, h, ROWS - 16:, :] = jnp.where(row16_part < 9, last_rows, ends).astype(BF16)

    a_copies = {}
    for h in range(PARTS):
        for d in (1, 2, 3, 0):
            chunk = (j + d) % PLANE
            state_part(d, chunk, h)
            if d:
                a_copies[d, h] = pltpu.make_async_remote_copy(
                    src_ref=local.at[d, h], dst_ref=from_plane.at[d, h],
                    send_sem=a_send.at[d, h], recv_sem=a_recv.at[d, h],
                    device_id={"seq": base + chunk}, device_id_type=MESH)
                a_copies[d, h].start()

    def turn_queries(tile, _):
        at = lanes(tile)
        scaled = mixed[:, at].astype(F32) * 0.25
        mixed[:, at] = scaled.astype(BF16)
        query_t[at, :] = scaled.T
        return 0

    lax.fori_loop(0, KEYS // 128, turn_queries, 0)

    def query_features(head, _):
        q = query_t[pl.ds(pl.multiple_of(head * 16, 16), 16), :]
        phi = features(q, 2.0, 2.0) * prior[0:1, :]
        phi = jnp.concatenate([phi, jnp.zeros((256 - ROWS, length), F32)], axis=0)
        phi_q[head] = phi.astype(BF16).T
        return 0

    def gathered(d, h):
        return local[0, h] if d == 0 else from_plane[d, h]

    b_copies = {}
    for h in range(PARTS):
        lax.fori_loop(h * 8, h * 8 + 8, query_features, 0)
        for d in range(1, PLANE):
            a_copies[d, h].wait_recv()
        total_sum = jnp.zeros((ROWS, 256), F32)
        for d in range(PLANE):
            source = (j - d + PLANE) % PLANE
            keep = jnp.where(opens[PLANE] < start_of(base + source + 1), 1.0, 0.0)
            total_sum = total_sum + gathered(d, h).astype(F32) * keep
        total[h] = total_sum.astype(BF16)
        for k in (1, 2):
            b_copies[k, h] = pltpu.make_async_remote_copy(
                src_ref=total.at[h], dst_ref=from_z.at[k - 1, h], send_sem=b_send.at[k - 1, h],
                recv_sem=b_recv.at[k - 1, h], device_id={"seq": me + k * PLANE},
                device_id_type=MESH)
            pl.when(z < planes - k)(b_copies[k, h].start)

    lax.fori_loop(16, HEADS, query_features, 0)

    key_row = lax.broadcasted_iota(jnp.int32, (128, 1), 0) // FEAT
    blocks = length // 128

    def attend(pair, _):
        tile = pair // 4
        v = values_at(pair)
        q = mixed[:, lanes(tile)]
        keys = key_t[lanes(tile), :]
        here = (pair % 4) * 2
        k_even = jnp.where(key_row == here, keys, 0.0).astype(BF16)
        k_odd = jnp.where(key_row == here + 1, keys, 0.0).astype(BF16)
        one, nil = jnp.ones((128, 128), BF16), jnp.zeros((128, 128), BF16)
        sums = []
        for b in range(blocks):
            part = slice(b * 128, b * 128 + 128)
            k = jnp.concatenate([k_even[:, part], k_odd[:, part]], axis=1)
            s = jnp.dot(q[b * 128:], k, preferred_element_type=F32) + 1.0
            w = (s * s + 1.0).astype(BF16) * causal[b * 128:, b * 256:b * 256 + 256]
            va = jnp.concatenate([
                jnp.concatenate([jnp.where(low, v[part], one), nil], axis=1),
                jnp.concatenate([nil, jnp.where(low, one, v[part])], axis=1)], axis=0)
            sums.append(jnp.dot(w, va, preferred_element_type=F32))
        for b in range(blocks):
            rows = slice(b * 128, b * 128 + 128)
            whole = sums[0][rows]
            for e in range(1, b + 1):
                whole = whole + sums[e][(b - e) * 128:(b - e) * 128 + 128]
            acc[pair, rows, :] = whole
        return 0

    c_copies = {}
    for h in range(PARTS):
        lax.fori_loop(h * 4, h * 4 + 4, attend, 0, unroll=2)
        for k in (1, 2):
            pl.when(z >= k)(b_copies[k, h].wait_recv)
        for d in (1, 2, 3, 0):
            to = (j + d) % PLANE
            open_at = opens[0]
            for i in range(1, PLANE):
                open_at = jnp.where(to == i, opens[i], open_at)
            state = from_z[0, h].astype(F32) * jnp.where(open_at < edge[PLANE], 1.0, 0.0)
            state = state + from_z[1, h].astype(F32) * jnp.where(open_at < edge[0], 1.0, 0.0)
            for e in range(PLANE):
                source = (j - e + PLANE) % PLANE
                keep = (source < to) & (open_at < start_of(base + source + 1))
                state = state + gathered(e, h).astype(F32) * jnp.where(keep, 1.0, 0.0)
            if d:
                carry_out[d, h] = state.astype(BF16)
                c_copies[d, h] = pltpu.make_async_remote_copy(
                    src_ref=carry_out.at[d, h], dst_ref=carried.at[d, h],
                    send_sem=c_send.at[d, h], recv_sem=c_recv.at[d, h],
                    device_id={"seq": base + to}, device_id_type=MESH)
                c_copies[d, h].start()
            else:
                carried[0, h] = state.astype(BF16)

    lax.fori_loop(PAIRS // 2, PAIRS, attend, 0, unroll=2)

    from_row = lax.broadcasted_iota(jnp.int32, (16, 512), 0)
    to_col = lax.broadcasted_iota(jnp.int32, (16, 512), 1)
    spread = jnp.where(from_row == 9 + to_col // 128, 1.0, 0.0).astype(BF16)
    pad = jnp.zeros((256 - ROWS, 128), BF16)
    for h, d in [(h, d) for h in range(PARTS) for d in range(PLANE)]:
        if d:
            c_copies[d, h].wait_recv()
        chunk = (j - d + PLANE) % PLANE
        norms = lax.dot_general(carried[d, h, ROWS - 16:, :], spread, (((0,), (0,)), ((), ())),
                                preferred_element_type=F32).astype(BF16)[:ROWS]
        for i in range(PER // PARTS):
            pair = chunk * PER + h * (PER // PARTS) + i
            values = carried[d, h, :, i * 128:i * 128 + 128]
            norm = norms[:, i * 256:i * 256 + 256]
            s_even = jnp.concatenate([jnp.where(low, values, norm[:, :128]), pad], axis=0)
            s_odd = jnp.concatenate([jnp.where(low, norm[:, 128:], values), pad], axis=0)
            mine = acc[pair]
            even = mine[:, :128] + jnp.dot(phi_q[pair * 2], s_even, preferred_element_type=F32)
            odd = mine[:, 128:] + jnp.dot(phi_q[pair * 2 + 1], s_odd, preferred_element_type=F32)
            numer = jnp.where(low, even, odd)
            denom = pltpu.roll(jnp.where(low, odd, even), 64, 1)
            good = denom != 0.0
            result = jnp.where(good, numer / jnp.where(good, denom, 1.0), 0.0)
            out[:, lanes(pair)] = result.astype(BF16)

    pl.when(me < n - 1)(halo_copy.wait_send)
    for h in range(PARTS):
        for d in range(1, PLANE):
            a_copies[d, h].wait_send()
            c_copies[d, h].wait_send()
        for k in (1, 2):
            pl.when(z < planes - k)(b_copies[k, h].wait_send)


def per_device(projected, conv_weight, doc_lengths, load_starts):
    n = lax.axis_size("seq")
    length, channels = projected.shape
    state = (PARTS, ROWS, PER // PARTS * 128)
    vmem = pl.BlockSpec(memory_space=pltpu.VMEM)
    smem = pl.BlockSpec(memory_space=pltpu.SMEM)
    return pl.pallas_call(
        functools.partial(kernel, n),
        out_shape=jax.ShapeDtypeStruct((length, HEADS * HEAD_DIM), BF16),
        in_specs=[pl.BlockSpec(memory_space=pl.ANY)] * 2 + [smem, smem],
        out_specs=vmem,
        scratch_shapes=[
            pltpu.VMEM((length, channels), BF16),
            pltpu.VMEM(conv_weight.shape, F32),
            pltpu.VMEM((length, channels), BF16),
            pltpu.VMEM((KEYS, length), F32),
            pltpu.VMEM((KEYS, length), F32),
            pltpu.VMEM((length, 128), F32),
            pltpu.VMEM((length, 128), F32),
            pltpu.VMEM((length, 128), BF16),
            pltpu.VMEM((8, length), F32),
            pltpu.VMEM((length, 2 * length), BF16),
            pltpu.VMEM((16, channels), BF16),
            pltpu.VMEM((16, channels), BF16),
            pltpu.VMEM((PLANE,) + state, BF16),
            pltpu.VMEM((PLANE,) + state, BF16),
            pltpu.VMEM(state, BF16),
            pltpu.VMEM((2,) + state, BF16),
            pltpu.VMEM((PLANE,) + state, BF16),
            pltpu.VMEM((PLANE,) + state, BF16),
            pltpu.VMEM((PAIRS, length, 256), F32),
            pltpu.VMEM((HEADS, length, 256), BF16),
            pltpu.SemaphoreType.DMA((2,)),
            pltpu.SemaphoreType.DMA((PLANE, PARTS)),
            pltpu.SemaphoreType.DMA((PLANE, PARTS)),
            pltpu.SemaphoreType.DMA((2, PARTS)),
            pltpu.SemaphoreType.DMA((2, PARTS)),
            pltpu.SemaphoreType.DMA((PLANE, PARTS)),
            pltpu.SemaphoreType.DMA((PLANE, PARTS)),
            pltpu.SemaphoreType.DMA((2,)),
        ],
        compiler_params=pltpu.CompilerParams(
            collective_id=0, has_side_effects=True, vmem_limit_bytes=60 * 1024 * 1024),
    )(projected, conv_weight, doc_lengths, load_starts)


def solution(mesh):
    return jax.shard_map(
        per_device,
        mesh=mesh,
        in_specs=(P(("groups", "seq"), None), P(), P("groups"), P("groups")),
        out_specs=P(("groups", "seq"), None),
        check_vma=False,
    )
```
